32 devices in a mesh: groups: 2 (over x), rows: 16 (over z, y, core).
Axes of the slice: x: 2, y: 2, z: 4, core: 2. Of those that a mesh axis runs over, the one named last changes fastest.
Arguments:
- depth: float32 [256, 1024], P(('groups', 'rows')), parts along dimension 0, may hold values from 0.02 to 3
- flux_x: float32 [256, 1024], P(('groups', 'rows')), parts along dimension 0, may hold values from -4 to 4
- flux_y: float32 [256, 1024], P(('groups', 'rows')), parts along dimension 0, may hold values from -4 to 4
- elevation: float32 [256, 1024], P(('groups', 'rows')), parts along dimension 0, may hold values from -6 to 6
- roughness: float32 [256, 1024], P(('groups', 'rows')), parts along dimension 0, may hold values from 0.02 to 0.1
- wet_tiles: int32 [32, 128], P(('groups', 'rows')), parts along dimension 0, may hold values 0 or 1
- chan_depth: float32 [1536, 128], P(('groups', 'rows')), parts along dimension 0, may hold values from 0.5 to 5
- chan_flow: float32 [1536, 128], P(('groups', 'rows')), parts along dimension 0, may hold values from -8 to 8
- chan_bed: float32 [1536, 128], P(('groups', 'rows')), parts along dimension 0, may hold values from -6 to 6
- chan_width: float32 [1536, 128], P(('groups', 'rows')), parts along dimension 0, may hold values from 20 to 200
- lateral_owner: int32 [1536, 1], P(('groups', 'rows')), parts along dimension 0, may hold values from 0 to 15; in each aligned block of 48 rows (0 to 47, 48 to 95, ...) at most 9 rows name the same one
- lateral_row: int32 [1536], P(('groups', 'rows')), parts along dimension 0, may hold values from 0 to 7
- reach_offset: int32 [1536], P(('groups', 'rows')), parts along dimension 0, may hold values from 0 to 896
Outputs:
- depth_out: float32 [256, 1024], P(('groups', 'rows')), parts along dimension 0
- flux_x_out: float32 [256, 1024], P(('groups', 'rows')), parts along dimension 0
- flux_y_out: float32 [256, 1024], P(('groups', 'rows')), parts along dimension 0
- chan_depth_out: float32 [1536, 128], P(('groups', 'rows')), parts along dimension 0
- chan_flow_out: float32 [1536, 128], P(('groups', 'rows')), parts along dimension 0
The draws below stay inside these ranges and needn't reach their ends.
There are 2 independent parts, one for each index of `groups`. The reference program is written for one: setup_inputs(seed, part) draws one part's arguments, and reference() takes and returns one part's arrays. A program takes and returns all parts, laid end to end along the dimension named above; each array names one. Nothing has to cross between parts.
Inputs may be any that keep to these rules, and one draw needn't show every extreme that they name: `lateral_owner`: among the 48 reaches of one device (aligned blocks), no device index is named more than 9 times.
All inputs are finite; a program needn't handle non-finite values. No bound on the sum of `wet_tiles` on one device may be relied on, other than what follows from the above.
Results may differ from the reference program's by a relative error of at most 0.00002.
Values sent between devices are 32-bit elements; how exact they have to be, the bound alone decides.
A program may use at most 64 MiB of HBM per device.

```python
import math
import jax
import jax.numpy as jnp
import numpy as np

RD = 8
COLS = 1024
TILE = 8
NODES = 128
REACH_DEV = 48
STEPS = 2
CAP = 9
NR = 128
REACHES = 768
N_ROWS = 16


def with_ends(values, key, least, high):
    spot = [jax.random.randint(jax.random.fold_in(key, axis), (), 0, length) for axis, length in enumerate(values.shape)]
    longest = values.shape.index(max(values.shape))
    neighbour = spot[:longest] + [(spot[longest] + 1) % values.shape[longest]] + spot[longest + 1:]
    return values.at[tuple(spot)].set(least).at[tuple(neighbour)].set(high)


def shard_levels(stream_key, extent, shards, smallest, high):
    def one(position, shards_of):
        heights = jax.random.uniform(jax.random.fold_in(jax.random.fold_in(stream_key, 6), position), (shards_of,), jnp.float32, smallest / len(shards), high / len(shards))
        return jnp.repeat(jnp.exp(heights), extent[position] // shards_of).reshape((-1,) + (1,) * (len(extent) - position - 1))

    factor_of = one(*shards[0])
    for cut in shards[1:]:
        factor_of = factor_of * one(*cut)
    return factor_of


def shared_out(own_key, own, number, rows, number_of, top, reach, skew):
    ranking = jax.random.permutation(own_key, number_of)
    crowded, ordinary = load_shares(number_of, rows * top, reach, skew, True), load_shares(number_of, rows * top, reach, skew, False)
    places = jnp.arange(number_of)

    def named(sizes, rotation):
        used = int((sizes > 0).sum())
        fixed = max(1, used // 4)
        shifted = fixed + (places - fixed + rotation * (used - fixed)) % max(1, number_of - fixed)
        return jnp.zeros((number_of,), jnp.int32).at[ranking[jnp.where(places < fixed, places, shifted)]].set(jnp.asarray(sizes, jnp.int32))

    sizes = jnp.where(number % 4 == 0, named(crowded, number // 4), named(ordinary, number - number // 4 - 1))
    mixed = jax.random.permutation(jax.random.fold_in(own, 3), number_of)
    donor, sink = mixed[0:number_of // 2 * 2:2], mixed[1:number_of // 2 * 2:2]
    room = jnp.minimum(sizes[donor] - 1, reach - sizes[sink]) // 2
    room = jnp.where((donor == ranking[0]) | (sink == ranking[0]) | (sizes[sink] == 0), 0, jnp.maximum(room, 0))
    shifted = jax.random.randint(jax.random.fold_in(own, 4), (number_of // 2,), 0, 1 << 20) % (room + 1)
    sizes = sizes.at[donor].add(-shifted).at[sink].add(shifted)
    items = jnp.searchsorted(jnp.cumsum(sizes), jnp.arange(rows * top), side="right").astype(jnp.int32)
    grid = items.reshape(top, rows).T
    grid = grid[jax.random.permutation(jax.random.fold_in(own, 1), rows)]
    rotation = jax.random.randint(jax.random.fold_in(own, 2), (rows, 1), 0, top)
    return jnp.take_along_axis(grid, (jnp.arange(top)[None, :] + rotation) % top, axis=1)


def load_shares(amount, total, limit, skew, full):
    portions = [(1 << 20) // math.isqrt(standing ** skew) + 1 for standing in range(1, amount + 1)]
    largest = limit if full else min(limit, max(-(-total // amount), total * portions[0] // sum(portions)))
    least = 1 if total - largest >= amount - 1 else 0
    holding, surplus = [largest] + [least] * (amount - 1), total - largest - least * (amount - 1)
    while surplus > 0:
        movable = [i for i in range(1, amount) if holding[i] < largest] or [i for i in range(1, amount) if holding[i] < limit]
        pool, left = sum([portions[i] for i in movable]), surplus
        for i in movable:
            more = min(limit - holding[i], max(1, left * portions[i] // pool), surplus)
            holding[i] = holding[i] + more
            surplus = surplus - more
    return np.array(holding)


def bell_draw(rng, dims, spread, bound, cuts=(), kind=jnp.bfloat16):
    entries = jax.random.normal(rng, dims, jnp.float32) * spread
    if len(cuts) > 0:
        entries = shard_levels(rng, dims, cuts, -0.22, 0.18) * entries
    return jnp.clip(entries, min=-bound, max=bound).astype(kind)


def setup_inputs(seed: int = 0, part: int = 0) -> dict:
    key_list = jax.random.split(jax.random.key(seed), 14)
    part_splits = jax.random.split(jax.random.fold_in(key_list[13], part), 14)
    depth = jnp.clip(jnp.exp(math.log(3.0) - 5.0106353 * jax.random.uniform(part_splits[0], (NR, COLS), jnp.float32) ** shard_levels(part_splits[0], (NR, COLS), ((0, 16),), -0.2, 0.2)), 0.02, 3.0)
    flux_x = bell_draw(part_splits[1], (NR, COLS), 0.5, 4.0, ((0, 16),), jnp.float32)
    flux_y = bell_draw(part_splits[2], (NR, COLS), 0.5, 4.0, ((0, 16),), jnp.float32)
    elevation = bell_draw(part_splits[3], (NR, COLS), 1.0, 6.0, ((0, 16),), jnp.float32)
    roughness = jnp.clip(jnp.exp(math.log(0.1) - 1.609438 * jax.random.uniform(part_splits[4], (NR, COLS), jnp.float32) ** shard_levels(part_splits[4], (NR, COLS), ((0, 16),), -0.2, 0.2)), 0.02, 0.1)
    wet_tiles = with_ends((jax.random.randint(part_splits[5], (NR // TILE, COLS // TILE), 0, 4) < 1).astype(jnp.int32), jax.random.fold_in(part_splits[5], 1), 0, 1)
    chan_depth = jnp.clip(jnp.exp(math.log(5.0) - 2.3025851 * jax.random.uniform(part_splits[6], (REACHES, NODES), jnp.float32) ** shard_levels(part_splits[6], (REACHES, NODES), ((0, 16),), -0.2, 0.2)), 0.5, 5.0)
    chan_flow = bell_draw(part_splits[7], (REACHES, NODES), 2.0, 8.0, ((0, 16),), jnp.float32)
    chan_bed = bell_draw(part_splits[8], (REACHES, NODES), 1.0, 6.0, ((0, 16),), jnp.float32)
    chan_width = jnp.clip(jnp.exp(math.log(200.0) - 2.3025851 * jax.random.uniform(part_splits[9], (REACHES, NODES), jnp.float32) ** shard_levels(part_splits[9], (REACHES, NODES), ((0, 16),), -0.2, 0.2)), 20.0, 200.0)
    lateral_owner_keys = jax.random.split(jax.random.fold_in(part_splits[10], 1), REACHES // REACH_DEV)
    lateral_owner_turns = jax.random.permutation(jax.random.fold_in(part_splits[10], 3), REACHES // REACH_DEV)
    lateral_owner = jax.vmap(lambda own, number: shared_out(jax.random.fold_in(part_splits[10], 2), own, number, REACH_DEV, N_ROWS, 1, CAP, 2))(lateral_owner_keys, lateral_owner_turns).reshape((REACHES, 1))
    lateral_row = with_ends(jax.random.randint(part_splits[11], (REACHES,), 0, RD), jax.random.fold_in(part_splits[11], 1), 0, RD - 1).astype(jnp.int32)
    reach_offset = with_ends(jax.random.randint(part_splits[12], (REACHES,), 0, COLS - NODES + 1), jax.random.fold_in(part_splits[12], 1), 0, COLS - NODES).astype(jnp.int32)
    return dict(depth=depth, flux_x=flux_x, flux_y=flux_y, elevation=elevation, roughness=roughness, wet_tiles=wet_tiles, chan_depth=chan_depth, chan_flow=chan_flow, chan_bed=chan_bed, chan_width=chan_width, lateral_owner=lateral_owner, lateral_row=lateral_row, reach_offset=reach_offset)


GRAVITY = 9.81
TIME_STEP = 5.0
CELL_SIZE = 90.0
DEPTH_FLOOR = 0.05
EXCHANGE_COEF = 40.0
CHANNEL_MANNING = 0.035


def face_flux(flux, upper_a, upper_b, floor_a, floor_b, manning, active):
    flow_depth = jnp.maximum(jnp.maximum(upper_a, upper_b) - jnp.maximum(floor_a, floor_b), 0.0)
    slope = (upper_b - upper_a) / CELL_SIZE
    friction = jnp.maximum(flow_depth, DEPTH_FLOOR) ** (7.0 / 3.0)
    return active * (flux - GRAVITY * flow_depth * TIME_STEP * slope) / (1.0 + GRAVITY * TIME_STEP * manning * manning * jnp.abs(flux) / friction)


def reference(depth, flux_x, flux_y, elevation, roughness, wet_tiles, chan_depth, chan_flow, chan_bed, chan_width, lateral_owner, lateral_row, reach_offset):
    wetness = jnp.repeat(jnp.repeat(wet_tiles, TILE, axis=0), TILE, axis=1).astype(jnp.float32)
    total_rows = depth.shape[0]
    col_zero = jnp.zeros((total_rows, 1), jnp.float32)
    row_zero = jnp.zeros((1, depth.shape[1]), jnp.float32)
    chan_zero = jnp.zeros((chan_depth.shape[0], 1), jnp.float32)
    active_x = jnp.maximum(wetness[:, :-1], wetness[:, 1:])
    active_y = jnp.maximum(wetness[:-1], wetness[1:])
    manning_x = 0.5 * (roughness[:, :-1] + roughness[:, 1:])
    manning_y = 0.5 * (roughness[:-1] + roughness[1:])
    owner_rows = (lateral_owner[:, 0] * RD + lateral_row).astype(jnp.int32)
    node_cols = reach_offset[:, None].astype(jnp.int32) + jnp.arange(NODES, dtype=jnp.int32)[None, :]
    row_grid = jnp.broadcast_to(owner_rows[:, None], node_cols.shape)
    for iteration in range(STEPS):
        surface = elevation + depth
        new_x = face_flux(flux_x[:, :-1], surface[:, :-1], surface[:, 1:], elevation[:, :-1], elevation[:, 1:], manning_x, active_x)
        flux_x = jnp.concatenate([new_x, col_zero], axis=1)
        new_y = face_flux(flux_y[:-1], surface[:-1], surface[1:], elevation[:-1], elevation[1:], manning_y, active_y)
        flux_y = jnp.concatenate([new_y, row_zero], axis=0)
        chan_surface = chan_bed + chan_depth
        lateral = EXCHANGE_COEF * (chan_surface - surface[row_grid, node_cols])
        gained = jnp.zeros_like(depth).at[row_grid, node_cols].add(lateral)
        inflow = jnp.concatenate([col_zero, flux_x[:, :-1]], axis=1) - flux_x + jnp.concatenate([row_zero, flux_y[:-1]], axis=0) - flux_y
        depth = jnp.maximum(depth + TIME_STEP / CELL_SIZE * inflow + TIME_STEP * gained / (CELL_SIZE * CELL_SIZE), 0.0)
        new_c = face_flux(chan_flow[:, :-1], chan_surface[:, :-1], chan_surface[:, 1:], chan_bed[:, :-1], chan_bed[:, 1:], CHANNEL_MANNING, 1.0)
        chan_flow = jnp.concatenate([new_c, chan_zero], axis=1)
        chan_inflow = jnp.concatenate([chan_zero, chan_flow[:, :-1]], axis=1) - chan_flow
        chan_depth = jnp.maximum(chan_depth + TIME_STEP / CELL_SIZE * chan_inflow - TIME_STEP * lateral / (chan_width * CELL_SIZE), 0.0)
    return (depth, flux_x, flux_y, chan_depth, chan_flow)
```

```python
import functools

import jax
import jax.numpy as jnp
from jax import lax
from jax.experimental import pallas as pl
from jax.experimental.pallas import tpu as pltpu
from jax.sharding import PartitionSpec as P

TILE = 8
LANES = 128

GRAVITY = 9.81
TIME_STEP = 5.0
CELL_SIZE = 90.0
DEPTH_FLOOR = 0.05
EXCHANGE_COEF = 40.0
CHANNEL_MANNING = 0.035

F32 = jnp.float32
BF16 = jnp.bfloat16
MESH = pl.DeviceIdType.MESH


def face_flux(flux, upper_a, upper_b, floor_a, floor_b, manning, active):
    flow_depth = jnp.maximum(jnp.maximum(upper_a, upper_b) - jnp.maximum(floor_a, floor_b), 0.0)
    slope = (upper_b - upper_a) * (GRAVITY * TIME_STEP / CELL_SIZE)
    inverse = jnp.exp((-7.0 / 3.0) * jnp.log(jnp.maximum(flow_depth, DEPTH_FLOOR)))
    return (
        active
        * (flux - flow_depth * slope)
        / (1.0 + (GRAVITY * TIME_STEP) * manning * manning * jnp.abs(flux) * inverse)
    )


def iota(shape, axis):
    return lax.broadcasted_iota(jnp.int32, shape, axis)


def split3(x):
    high = x.astype(BF16)
    rest = x - high.astype(F32)
    mid = rest.astype(BF16)
    low = (rest - mid.astype(F32)).astype(BF16)
    return jnp.concatenate([high, mid, low], axis=1)


def join3(x):
    width = x.shape[1] // 3
    return (x[:, 2 * width :] + x[:, width : 2 * width]) + x[:, :width]


def pick(onehot, x):
    return join3(jnp.dot(onehot, split3(x), preferred_element_type=F32))


def pick_t(onehot, x):
    return join3(
        lax.dot_general(
            onehot, split3(x), (((0,), (0,)), ((), ())), preferred_element_type=F32
        )
    )


def roll_rows(x, amount, to_right):
    for bit in range(7):
        step = 1 << bit
        turned = pltpu.roll(x, step if to_right else LANES - step, 1)
        x = jnp.where((amount & step) != 0, turned, x)
    return x


def kernel(n, cap, cpad, *refs):
    (
        depth_h, fx_h, fy_h, el_h, ro_h, wet_h, cd_h, cf_h, cb_h, cw_h, own_h, row_h, off_h,
        depth_o, fx_o, fy_o, cd_o, cf_o,
        depth_v, fx_v, fy_v, el_v, ro_v, wet_v, cd_v, cf_v, cb_v, cw_v, own_v, row_v, off_v,
        depth_w, fx_w, fy_w, cd_w, cf_w,
        send_a, recv_a, send_b, recv_b, back_a, home_a, back_b, home_b,
        up_s, down_s, below_r, above_r, up2_s, down2_s, below2_r, above2_r,
        in_sem, out_sem, sa, ra, sb, rb, sc, rc, sd, rd, hs, hr,
    ) = refs
    me = lax.axis_index("rows")
    rows, columns = depth_v.shape
    blocks = columns // LANES
    cells = rows * blocks
    reaches, nodes = cd_v.shape
    slots = n * cpad

    inputs = [
        pltpu.make_async_copy(h, v, in_sem.at[i])
        for i, (h, v) in enumerate(
            [
                (own_h, own_v), (row_h, row_v), (off_h, off_v), (cb_h, cb_v), (cd_h, cd_v),
                (depth_h, depth_v), (el_h, el_v), (ro_h, ro_v), (fy_h, fy_v), (wet_h, wet_v),
                (cf_h, cf_v), (cw_h, cw_v), (fx_h, fx_v),
            ]
        )
    ]
    for copy in inputs:
        copy.start()

    for ref in (recv_a, recv_b, home_a, home_b):
        ref[...] = jnp.zeros_like(ref)

    barrier = pltpu.get_barrier_semaphore()

    def greet(k, _):
        pl.semaphore_signal(
            barrier, inc=1, device_id={"rows": lax.rem(me + k, n)}, device_id_type=MESH
        )
        return _

    lax.fori_loop(1, n, greet, 0)

    for copy in inputs[:5]:
        copy.wait()
    owner_r = own_v[...]
    offset_r = off_v[...]
    key_r = (offset_r >> 7) * rows + row_v[...]
    turn_r = offset_r & (LANES - 1)
    ri, ci = iota((reaches, reaches), 0), iota((reaches, reaches), 1)

    def column(v):
        wide = jnp.broadcast_to(v.astype(F32), (reaches, reaches))
        return jnp.sum(jnp.where(ri == ci, wide, 0.0), axis=1, keepdims=True)

    owner_f = owner_r.astype(F32)
    owner_c, key_c, turn_c = column(owner_r), column(key_r), column(turn_r)
    same = jnp.where(owner_c == owner_f, 1.0, 0.0)
    rank_c = jnp.sum(jnp.where(ci < ri, same, 0.0), axis=1, keepdims=True)
    rank_r = jnp.sum(jnp.where(ri < ci, same, 0.0), axis=0, keepdims=True)
    slot_r = (owner_f * cpad + rank_r).astype(jnp.int32)
    slot_c = (owner_c * cpad + rank_c).astype(jnp.int32)
    pack = jnp.where(iota((slots, reaches), 0) == slot_r, 1.0, 0.0).astype(BF16)
    unpack = jnp.where(iota((reaches, slots), 1) == slot_c, 1.0, 0.0).astype(BF16)

    bed = cb_v[...]
    cdepth = cd_v[...]
    csurf = bed + cdepth
    send_a[...] = pick(pack, csurf).reshape(n, cpad, nodes)
    lane = iota((reaches, LANES), 1)
    rank_i = rank_c.astype(jnp.int32)
    ids = jnp.where(
        lane == rank_i, key_c + 1.0, jnp.where(lane == rank_i + 64, turn_c, 0.0)
    ).astype(BF16)
    to_owner = jnp.where(iota((n, reaches), 0) == owner_r, 1.0, 0.0).astype(BF16)
    id_rows = jnp.dot(to_owner, ids, preferred_element_type=F32)
    for d in range(n):
        send_a[d, cap : cap + 1, :] = id_rows[d : d + 1, :]

    for copy in inputs[5:10]:
        copy.wait()
    depth, el, ro = depth_v[...], el_v[...], ro_v[...]
    fy = fy_v[...]
    tiles = wet_v[...].astype(F32)
    last = rows - 1
    up_s[0:1, :] = depth[0:1]
    up_s[1:2, :] = el[0:1]
    up_s[2:3, :] = ro[0:1]
    up_s[3:4, :] = fy[0:1]
    up_s[4:5, :] = jnp.zeros((1, columns), F32)
    up_s[4:5, 0 : tiles.shape[1]] = tiles
    down_s[0:1, :] = depth[last:]
    down_s[1:2, :] = el[last:]
    down_s[2:3, :] = ro[last:]
    down_s[3:4, :] = fy[last:]
    down_s[4:5, :] = jnp.zeros((1, columns), F32)
    down_s[4:5, 0 : tiles.shape[1]] = tiles

    def exchange(source, target, span, send_sem, recv_sem):
        def make(k):
            peer = lax.rem(me + k, n)
            return pltpu.make_async_remote_copy(
                src_ref=source.at[(peer,) + span],
                dst_ref=target.at[(me,) + span],
                send_sem=send_sem.at[k],
                recv_sem=recv_sem.at[k],
                device_id={"rows": peer},
                device_id_type=MESH,
            )

        def start():
            def one(k, _):
                make(k).start()
                return _

            lax.fori_loop(1, n, one, 0)
            target[me] = source[me]

        def arrive():
            def one(k, _):
                make(k).wait_recv()
                return _

            lax.fori_loop(1, n, one, 0)

        def leave():
            def one(k, _):
                make(k).wait_send()
                return _

            lax.fori_loop(1, n, one, 0)

        return start, arrive, leave

    a_span = (pl.ds(0, cap + 1),)
    b_span = (slice(None), pl.ds(0, cap))
    v_span = (pl.ds(0, cap),)
    start_a, arrive_a, leave_a = exchange(send_a, recv_a, a_span, sa, ra)
    start_b, arrive_b, leave_b = exchange(send_b, recv_b, b_span, sb, rb)
    start_c, arrive_c, leave_c = exchange(back_a, home_a, v_span, sc, rc)
    start_d, arrive_d, leave_d = exchange(back_b, home_b, v_span, sd, rd)

    above, below = lax.rem(me + n - 1, n), lax.rem(me + 1, n)

    def halo(src, dst, i, peer):
        return pltpu.make_async_remote_copy(
            src_ref=src, dst_ref=dst, send_sem=hs.at[i], recv_sem=hr.at[i],
            device_id={"rows": peer}, device_id_type=MESH,
        )

    halos = [halo(up_s, below_r, 0, above), halo(down_s, above_r, 1, below)]
    halos2 = [halo(up2_s, below2_r, 2, above), halo(down2_s, above2_r, 3, below)]

    pl.semaphore_wait(barrier, n - 1)
    start_a()
    for copy in halos:
        copy.start()

    for copy in inputs[10:]:
        copy.wait()
    node = iota((reaches, nodes), 1)
    inner = jnp.where(node < nodes - 1, 1.0, 0.0)
    bed_next = pltpu.roll(bed, nodes - 1, 1)

    def channel_flow(flow, surface):
        return face_flux(
            flow, surface, pltpu.roll(surface, nodes - 1, 1), bed, bed_next,
            CHANNEL_MANNING, inner,
        )

    def channel_inflow(flow):
        return (TIME_STEP / CELL_SIZE) * (pltpu.roll(flow, 1, 1) - flow)

    cflow = channel_flow(cf_v[...], csurf)
    cpart = cdepth + channel_inflow(cflow)
    per_width = TIME_STEP / (cw_v[...] * CELL_SIZE)
    send_b[:, 0] = pick(pack, bed).reshape(n, cpad, nodes)
    send_b[:, 1] = pick(pack, cpart).reshape(n, cpad, nodes)
    send_b[:, 2] = pick(pack, per_width).reshape(n, cpad, nodes)
    start_b()

    col = iota((rows, columns), 1)
    row = iota((rows, columns), 0)
    spread = jnp.where(
        iota((tiles.shape[1], columns), 0) == iota((tiles.shape[1], columns), 1) // TILE, 1.0, 0.0
    ).astype(BF16)

    def expand(t):
        wide = jnp.broadcast_to(t, (rows, t.shape[1])).astype(BF16)
        return jnp.dot(wide, spread, preferred_element_type=F32)

    wet = expand(tiles)
    el_right = pltpu.roll(el, columns - 1, 1)
    man_x = 0.5 * (ro + pltpu.roll(ro, columns - 1, 1))
    act_x = jnp.where(
        col < columns - 1, jnp.maximum(wet, pltpu.roll(wet, columns - 1, 1)), 0.0
    )

    def flood_x(flux, surface):
        return face_flux(
            flux, surface, pltpu.roll(surface, columns - 1, 1), el, el_right, man_x, act_x
        )

    def to_cells(x):
        return jnp.concatenate([x[:, b * LANES : (b + 1) * LANES] for b in range(blocks)], axis=0)

    def to_grid(x):
        return jnp.concatenate([x[b * rows : (b + 1) * rows] for b in range(blocks)], axis=1)

    surface = el + depth
    fx = flood_x(fx_v[...], surface)

    for copy in halos:
        copy.wait_recv()

    def shift_up(x, edge):
        return jnp.where(row == last, edge, pltpu.roll(x, rows - 1, 0))

    def shift_down(x, edge):
        return jnp.where(row == 0, edge, pltpu.roll(x, 1, 0))

    edge_below = jnp.where(me == n - 1, 0.0, 1.0)
    edge_above = jnp.where(me == 0, 0.0, 1.0)
    wet_below = expand(below_r[4:5, 0 : tiles.shape[1]])
    wet_above = expand(above_r[4:5, 0 : tiles.shape[1]])[0:1]
    el_below = below_r[1:2, :]
    el_down = shift_up(el, el_below)
    man_y = 0.5 * (ro + shift_up(ro, below_r[2:3, :]))
    act_y = jnp.where(row == last, edge_below, 1.0) * jnp.maximum(wet, wet_below * 1.0)
    act_y = jnp.where(row == last, act_y, wet)
    el_above = above_r[1:2, :]
    man_top = 0.5 * (above_r[2:3, :] + ro[0:1])
    act_top = edge_above * jnp.maximum(wet_above, wet[0:1])

    def flood_y(flux, top, surface, below_row, above_row):
        new = face_flux(
            flux, surface, shift_up(surface, below_row), el, el_down, man_y, act_y
        )
        new_top = face_flux(top, above_row, surface[0:1], el_above, el[0:1], man_top, act_top)
        return new, new_top

    fy, top = flood_y(
        fy, above_r[3:4, :], surface, el_below + below_r[0:1, :], el_above + above_r[0:1, :]
    )

    def inflow(fx, fy, top):
        return (TIME_STEP / CELL_SIZE) * (
            pltpu.roll(fx, 1, 1) - fx + shift_down(fy, top) - fy
        )

    part = depth + inflow(fx, fy, top)

    arrive_a()
    packed = recv_a[...]
    wide_ids = jnp.broadcast_to(packed[:, cap : cap + 1, :], (n, cpad, LANES))
    mine = (iota((n, cpad, LANES), 2) & 63) == iota((n, cpad, LANES), 1)
    kept = jnp.where(mine, wide_ids, 0.0).reshape(slots, LANES).astype(BF16)
    halves = jnp.where(
        (iota((LANES, 2 * LANES), 0) < 64) == (iota((LANES, 2 * LANES), 1) < LANES), 1.0, 0.0
    ).astype(BF16)
    decoded = jnp.dot(kept, halves, preferred_element_type=F32).astype(jnp.int32)
    key = decoded[:, :LANES] - 1
    turn = decoded[:, LANES:]
    cell = iota((slots, cells), 1)
    key_cells = key[:, :cells]
    first = jnp.where(cell == key_cells, 1.0, 0.0).astype(BF16)
    second = jnp.where(
        (cell == key_cells + rows) & (key_cells >= 0), 1.0, 0.0
    ).astype(BF16)
    both = jnp.concatenate([first, second], axis=0)
    right = iota((slots, LANES), 1) >= turn

    def windows(surface):
        found = pick(both, to_cells(surface))
        return roll_rows(jnp.where(right, found[:slots], found[slots:]), turn, False)

    def gains(lateral):
        turned = roll_rows(lateral, turn, True)
        halves = jnp.concatenate(
            [jnp.where(right, turned, 0.0), jnp.where(right, 0.0, turned)], axis=0
        )
        return (TIME_STEP / (CELL_SIZE * CELL_SIZE)) * to_grid(pick_t(both, halves))

    csurf_s = packed.reshape(slots, nodes)
    lateral = EXCHANGE_COEF * (csurf_s - windows(surface))
    back_a[...] = lateral.reshape(n, cpad, nodes)
    start_c()
    depth = jnp.maximum(part + gains(lateral), 0.0)
    up2_s[...] = depth[0:1]
    down2_s[...] = depth[last:]
    for copy in halos2:
        copy.start()

    surface = el + depth
    found = windows(surface)
    arrive_b()
    bed_s = recv_b[:, 0].reshape(slots, nodes)
    cpart_s = recv_b[:, 1].reshape(slots, nodes)
    width_s = recv_b[:, 2].reshape(slots, nodes)
    lateral2 = EXCHANGE_COEF * (bed_s + jnp.maximum(cpart_s - lateral * width_s, 0.0) - found)
    back_b[...] = lateral2.reshape(n, cpad, nodes)
    start_d()
    gained = gains(lateral2)

    fx = flood_x(fx, surface)
    fx_w[...] = fx
    for copy in halos2:
        copy.wait_recv()
    fy, top = flood_y(fy, top, surface, el_below + below2_r[...], el_above + above2_r[...])
    fy_w[...] = fy
    depth_w[...] = jnp.maximum(depth + inflow(fx, fy, top) + gained, 0.0)
    outs = [
        pltpu.make_async_copy(v, h, out_sem.at[i])
        for i, (v, h) in enumerate(
            [(depth_w, depth_o), (fx_w, fx_o), (fy_w, fy_o), (cf_w, cf_o), (cd_w, cd_o)]
        )
    ]
    for copy in outs[:3]:
        copy.start()

    arrive_c()
    cdepth = jnp.maximum(
        cpart - per_width * pick(unpack, home_a[...].reshape(slots, nodes)), 0.0
    )
    cflow = channel_flow(cflow, bed + cdepth)
    cf_w[...] = cflow
    outs[3].start()
    cpart = cdepth + channel_inflow(cflow)
    arrive_d()
    cd_w[...] = jnp.maximum(
        cpart - per_width * pick(unpack, home_b[...].reshape(slots, nodes)), 0.0
    )
    outs[4].start()

    leave_a()
    leave_b()
    leave_c()
    leave_d()
    for copy in halos + halos2:
        copy.wait_send()
    for copy in outs:
        copy.wait()


def per_device(
    depth, flux_x, flux_y, elevation, roughness, wet_tiles, chan_depth, chan_flow, chan_bed,
    chan_width, lateral_owner, lateral_row, reach_offset,
):
    n = lax.axis_size("rows")
    rows, columns = depth.shape
    reaches, nodes = chan_depth.shape
    cap = max(2, (3 * reaches + n - 1) // n)
    cpad = -(-(cap + 1) // 8) * 8
    operands = (
        depth, flux_x, flux_y, elevation, roughness, wet_tiles, chan_depth, chan_flow,
        chan_bed, chan_width, lateral_owner.reshape(1, reaches),
        lateral_row.reshape(1, reaches), reach_offset.reshape(1, reaches),
    )
    grid_like = jax.ShapeDtypeStruct((rows, columns), F32)
    chan_like = jax.ShapeDtypeStruct((reaches, nodes), F32)
    block = pltpu.VMEM((n, cpad, nodes), F32)
    triple = pltpu.VMEM((n, 3, cpad, nodes), F32)
    halo = pltpu.VMEM((5, columns), F32)
    line = pltpu.VMEM((1, columns), F32)
    dma = pltpu.SemaphoreType.DMA
    grid_v = pltpu.VMEM((rows, columns), F32)
    chan_v = pltpu.VMEM((reaches, nodes), F32)
    return pl.pallas_call(
        functools.partial(kernel, n, cap, cpad),
        out_shape=(grid_like, grid_like, grid_like, chan_like, chan_like),
        in_specs=[pl.BlockSpec(memory_space=pl.ANY)] * len(operands),
        out_specs=[pl.BlockSpec(memory_space=pl.ANY)] * 5,
        scratch_shapes=[pltpu.VMEM(x.shape, x.dtype) for x in operands]
        + [grid_v, grid_v, grid_v, chan_v, chan_v]
        + [block, block, triple, triple, block, block, block, block]
        + [halo] * 4
        + [line] * 4
        + [dma((13,)), dma((5,))]
        + [dma((n,))] * 8
        + [dma((4,)), dma((4,))],
        compiler_params=pltpu.CompilerParams(
            collective_id=0, has_side_effects=True, vmem_limit_bytes=32 * 1024 * 1024
        ),
    )(*operands)


def solution(mesh):
    spec2 = P(("groups", "rows"), None)
    spec1 = P(("groups", "rows"))
    return jax.shard_map(
        per_device,
        mesh=mesh,
        in_specs=(spec2,) * 11 + (spec1,) * 2,
        out_specs=(spec2,) * 5,
        check_vma=False,
    )
```

```python
import functools

import jax
import jax.numpy as jnp
from jax import lax
from jax.experimental import pallas as pl
from jax.experimental.pallas import tpu as pltpu
from jax.sharding import PartitionSpec as P

TILE = 8
LANES = 128

GRAVITY = 9.81
TIME_STEP = 5.0
CELL_SIZE = 90.0
DEPTH_FLOOR = 0.05
EXCHANGE_COEF = 40.0
CHANNEL_MANNING = 0.035

F32 = jnp.float32
BF16 = jnp.bfloat16
MESH = pl.DeviceIdType.MESH


def face_flux(flux, upper_a, upper_b, floor_a, floor_b, manning, active):
    flow_depth = jnp.maximum(jnp.maximum(upper_a, upper_b) - jnp.maximum(floor_a, floor_b), 0.0)
    slope = (upper_b - upper_a) * (GRAVITY * TIME_STEP / CELL_SIZE)
    inverse = jnp.exp((-7.0 / 3.0) * jnp.log(jnp.maximum(flow_depth, DEPTH_FLOOR)))
    return (
        active
        * (flux - flow_depth * slope)
        / (1.0 + (GRAVITY * TIME_STEP) * manning * manning * jnp.abs(flux) * inverse)
    )


def iota(shape, axis):
    return lax.broadcasted_iota(jnp.int32, shape, axis)


def split3(x):
    high = x.astype(BF16)
    rest = x - high.astype(F32)
    mid = rest.astype(BF16)
    low = (rest - mid.astype(F32)).astype(BF16)
    return jnp.concatenate([high, mid, low], axis=1)


def join3(x):
    width = x.shape[1] // 3
    return (x[:, 2 * width :] + x[:, width : 2 * width]) + x[:, :width]


def pick(onehot, x):
    return join3(jnp.dot(onehot, split3(x), preferred_element_type=F32))


def pick_t(onehot, x):
    return join3(
        lax.dot_general(
            onehot, split3(x), (((0,), (0,)), ((), ())), preferred_element_type=F32
        )
    )


def roll_rows(x, amount, to_right):
    for bit in range(7):
        step = 1 << bit
        turned = pltpu.roll(x, step if to_right else LANES - step, 1)
        x = jnp.where((amount & step) != 0, turned, x)
    return x


def kernel(n, cap, cpad, *refs):
    (
        depth_h, fx_h, fy_h, el_h, ro_h, wet_h, cd_h, cf_h, cb_h, cw_h, own_h, row_h, off_h,
        depth_w, fx_w, fy_w, cd_w, cf_w,
        depth_v, fx_v, fy_v, el_v, ro_v, wet_v, cd_v, cf_v, cb_v, cw_v, own_v, row_v, off_v,
        send_a, recv_a, send_b, recv_b, back_a, home_a, back_b, home_b,
        up_s, down_s, below_r, above_r, up2_s, down2_s, below2_r, above2_r,
        in_sem, sa, ra, sb, rb, sc, rc, sd, rd, hs, hr,
    ) = refs
    me = lax.axis_index("rows")
    rows, columns = depth_v.shape
    blocks = columns // LANES
    cells = rows * blocks
    reaches, nodes = cd_v.shape
    slots = n * cpad

    inputs = [
        pltpu.make_async_copy(h, v, in_sem.at[i])
        for i, (h, v) in enumerate(
            [
                (own_h, own_v), (row_h, row_v), (off_h, off_v), (cb_h, cb_v), (cd_h, cd_v),
                (depth_h, depth_v), (el_h, el_v), (ro_h, ro_v), (fy_h, fy_v), (wet_h, wet_v),
                (cf_h, cf_v), (cw_h, cw_v), (fx_h, fx_v),
            ]
        )
    ]
    for copy in inputs:
        copy.start()

    for ref in (recv_a, recv_b, home_a, home_b):
        ref[...] = jnp.zeros_like(ref)

    barrier = pltpu.get_barrier_semaphore()

    def greet(k, _):
        pl.semaphore_signal(
            barrier, inc=1, device_id={"rows": lax.rem(me + k, n)}, device_id_type=MESH
        )
        return _

    lax.fori_loop(1, n, greet, 0)

    for copy in inputs[:5]:
        copy.wait()
    owner_r = own_v[...]
    offset_r = off_v[...]
    key_r = (offset_r >> 7) * rows + row_v[...]
    turn_r = offset_r & (LANES - 1)
    ri, ci = iota((reaches, reaches), 0), iota((reaches, reaches), 1)

    def column(v):
        wide = jnp.broadcast_to(v.astype(F32), (reaches, reaches))
        return jnp.sum(jnp.where(ri == ci, wide, 0.0), axis=1, keepdims=True)

    owner_f = owner_r.astype(F32)
    owner_c, key_c, turn_c = column(owner_r), column(key_r), column(turn_r)
    same = jnp.where(owner_c == owner_f, 1.0, 0.0)
    rank_c = jnp.sum(jnp.where(ci < ri, same, 0.0), axis=1, keepdims=True)
    rank_r = jnp.sum(jnp.where(ri < ci, same, 0.0), axis=0, keepdims=True)
    slot_r = (owner_f * cpad + rank_r).astype(jnp.int32)
    slot_c = (owner_c * cpad + rank_c).astype(jnp.int32)
    pack = jnp.where(iota((slots, reaches), 0) == slot_r, 1.0, 0.0).astype(BF16)
    unpack = jnp.where(iota((reaches, slots), 1) == slot_c, 1.0, 0.0).astype(BF16)

    bed = cb_v[...]
    cdepth = cd_v[...]
    csurf = bed + cdepth
    send_a[...] = pick(pack, csurf).reshape(n, cpad, nodes)
    lane = iota((reaches, LANES), 1)
    rank_i = rank_c.astype(jnp.int32)
    ids = jnp.where(
        lane == rank_i, key_c + 1.0, jnp.where(lane == rank_i + 64, turn_c, 0.0)
    ).astype(BF16)
    to_owner = jnp.where(iota((n, reaches), 0) == owner_r, 1.0, 0.0).astype(BF16)
    id_rows = jnp.dot(to_owner, ids, preferred_element_type=F32)
    for d in range(n):
        send_a[d, cap : cap + 1, :] = id_rows[d : d + 1, :]

    for copy in inputs[5:10]:
        copy.wait()
    depth, el, ro = depth_v[...], el_v[...], ro_v[...]
    fy = fy_v[...]
    tiles = wet_v[...].astype(F32)
    last = rows - 1
    up_s[0:1, :] = depth[0:1]
    up_s[1:2, :] = el[0:1]
    up_s[2:3, :] = ro[0:1]
    up_s[3:4, :] = fy[0:1]
    up_s[4:5, :] = jnp.zeros((1, columns), F32)
    up_s[4:5, 0 : tiles.shape[1]] = tiles
    down_s[0:1, :] = depth[last:]
    down_s[1:2, :] = el[last:]
    down_s[2:3, :] = ro[last:]
    down_s[3:4, :] = fy[last:]
    down_s[4:5, :] = jnp.zeros((1, columns), F32)
    down_s[4:5, 0 : tiles.shape[1]] = tiles

    def exchange(source, target, span, send_sem, recv_sem):
        def make(k):
            peer = lax.rem(me + k, n)
            return pltpu.make_async_remote_copy(
                src_ref=source.at[(peer,) + span],
                dst_ref=target.at[(me,) + span],
                send_sem=send_sem.at[k],
                recv_sem=recv_sem.at[k],
                device_id={"rows": peer},
                device_id_type=MESH,
            )

        def start():
            def one(k, _):
                make(k).start()
                return _

            lax.fori_loop(1, n, one, 0)
            target[me] = source[me]

        def arrive():
            def one(k, _):
                make(k).wait_recv()
                return _

            lax.fori_loop(1, n, one, 0)

        def leave():
            def one(k, _):
                make(k).wait_send()
                return _

            lax.fori_loop(1, n, one, 0)

        return start, arrive, leave

    a_span = (pl.ds(0, cap + 1),)
    b_span = (slice(None), pl.ds(0, cap))
    v_span = (pl.ds(0, cap),)
    start_a, arrive_a, leave_a = exchange(send_a, recv_a, a_span, sa, ra)
    start_b, arrive_b, leave_b = exchange(send_b, recv_b, b_span, sb, rb)
    start_c, arrive_c, leave_c = exchange(back_a, home_a, v_span, sc, rc)
    start_d, arrive_d, leave_d = exchange(back_b, home_b, v_span, sd, rd)

    above, below = lax.rem(me + n - 1, n), lax.rem(me + 1, n)

    def halo(src, dst, i, peer):
        return pltpu.make_async_remote_copy(
            src_ref=src, dst_ref=dst, send_sem=hs.at[i], recv_sem=hr.at[i],
            device_id={"rows": peer}, device_id_type=MESH,
        )

    halos = [halo(up_s, below_r, 0, above), halo(down_s, above_r, 1, below)]
    halos2 = [halo(up2_s, below2_r, 2, above), halo(down2_s, above2_r, 3, below)]

    pl.semaphore_wait(barrier, n - 1)
    start_a()
    for copy in halos:
        copy.start()

    for copy in inputs[10:]:
        copy.wait()
    node = iota((reaches, nodes), 1)
    inner = jnp.where(node < nodes - 1, 1.0, 0.0)
    bed_next = pltpu.roll(bed, nodes - 1, 1)

    def channel_flow(flow, surface):
        return face_flux(
            flow, surface, pltpu.roll(surface, nodes - 1, 1), bed, bed_next,
            CHANNEL_MANNING, inner,
        )

    def channel_inflow(flow):
        return (TIME_STEP / CELL_SIZE) * (pltpu.roll(flow, 1, 1) - flow)

    cflow = channel_flow(cf_v[...], csurf)
    cpart = cdepth + channel_inflow(cflow)
    per_width = TIME_STEP / (cw_v[...] * CELL_SIZE)
    send_b[:, 0] = pick(pack, bed).reshape(n, cpad, nodes)
    send_b[:, 1] = pick(pack, cpart).reshape(n, cpad, nodes)
    send_b[:, 2] = pick(pack, per_width).reshape(n, cpad, nodes)
    start_b()

    col = iota((rows, columns), 1)
    row = iota((rows, columns), 0)
    spread = jnp.where(
        iota((tiles.shape[1], columns), 0) == iota((tiles.shape[1], columns), 1) // TILE, 1.0, 0.0
    ).astype(BF16)

    def expand(t):
        wide = jnp.broadcast_to(t, (rows, t.shape[1])).astype(BF16)
        return jnp.dot(wide, spread, preferred_element_type=F32)

    wet = expand(tiles)
    el_right = pltpu.roll(el, columns - 1, 1)
    man_x = 0.5 * (ro + pltpu.roll(ro, columns - 1, 1))
    act_x = jnp.where(
        col < columns - 1, jnp.maximum(wet, pltpu.roll(wet, columns - 1, 1)), 0.0
    )

    def flood_x(flux, surface):
        return face_flux(
            flux, surface, pltpu.roll(surface, columns - 1, 1), el, el_right, man_x, act_x
        )

    def to_cells(x):
        return jnp.concatenate([x[:, b * LANES : (b + 1) * LANES] for b in range(blocks)], axis=0)

    def to_grid(x):
        return jnp.concatenate([x[b * rows : (b + 1) * rows] for b in range(blocks)], axis=1)

    surface = el + depth
    fx = flood_x(fx_v[...], surface)

    for copy in halos:
        copy.wait_recv()

    def shift_up(x, edge):
        return jnp.where(row == last, edge, pltpu.roll(x, rows - 1, 0))

    def shift_down(x, edge):
        return jnp.where(row == 0, edge, pltpu.roll(x, 1, 0))

    edge_below = jnp.where(me == n - 1, 0.0, 1.0)
    edge_above = jnp.where(me == 0, 0.0, 1.0)
    wet_below = expand(below_r[4:5, 0 : tiles.shape[1]])
    wet_above = expand(above_r[4:5, 0 : tiles.shape[1]])[0:1]
    el_below = below_r[1:2, :]
    el_down = shift_up(el, el_below)
    man_y = 0.5 * (ro + shift_up(ro, below_r[2:3, :]))
    act_y = jnp.where(row == last, edge_below, 1.0) * jnp.maximum(wet, wet_below * 1.0)
    act_y = jnp.where(row == last, act_y, wet)
    el_above = above_r[1:2, :]
    man_top = 0.5 * (above_r[2:3, :] + ro[0:1])
    act_top = edge_above * jnp.maximum(wet_above, wet[0:1])

    def flood_y(flux, top, surface, below_row, above_row):
        new = face_flux(
            flux, surface, shift_up(surface, below_row), el, el_down, man_y, act_y
        )
        new_top = face_flux(top, above_row, surface[0:1], el_above, el[0:1], man_top, act_top)
        return new, new_top

    fy, top = flood_y(
        fy, above_r[3:4, :], surface, el_below + below_r[0:1, :], el_above + above_r[0:1, :]
    )

    def inflow(fx, fy, top):
        return (TIME_STEP / CELL_SIZE) * (
            pltpu.roll(fx, 1, 1) - fx + shift_down(fy, top) - fy
        )

    part = depth + inflow(fx, fy, top)

    arrive_a()
    packed = recv_a[...]
    wide_ids = jnp.broadcast_to(packed[:, cap : cap + 1, :], (n, cpad, LANES))
    mine = (iota((n, cpad, LANES), 2) & 63) == iota((n, cpad, LANES), 1)
    kept = jnp.where(mine, wide_ids, 0.0).reshape(slots, LANES).astype(BF16)
    halves = jnp.where(
        (iota((LANES, 2 * LANES), 0) < 64) == (iota((LANES, 2 * LANES), 1) < LANES), 1.0, 0.0
    ).astype(BF16)
    decoded = jnp.dot(kept, halves, preferred_element_type=F32).astype(jnp.int32)
    key = decoded[:, :LANES] - 1
    turn = decoded[:, LANES:]
    cell = iota((slots, cells), 1)
    key_cells = key[:, :cells]
    first = jnp.where(cell == key_cells, 1.0, 0.0).astype(BF16)
    second = jnp.where(
        (cell == key_cells + rows) & (key_cells >= 0), 1.0, 0.0
    ).astype(BF16)
    both = jnp.concatenate([first, second], axis=0)
    right = iota((slots, LANES), 1) >= turn

    def windows(surface):
        found = pick(both, to_cells(surface))
        return roll_rows(jnp.where(right, found[:slots], found[slots:]), turn, False)

    def gains(lateral):
        turned = roll_rows(lateral, turn, True)
        halves = jnp.concatenate(
            [jnp.where(right, turned, 0.0), jnp.where(right, 0.0, turned)], axis=0
        )
        return (TIME_STEP / (CELL_SIZE * CELL_SIZE)) * to_grid(pick_t(both, halves))

    csurf_s = packed.reshape(slots, nodes)
    lateral = EXCHANGE_COEF * (csurf_s - windows(surface))
    back_a[...] = lateral.reshape(n, cpad, nodes)
    start_c()
    depth = jnp.maximum(part + gains(lateral), 0.0)
    up2_s[...] = depth[0:1]
    down2_s[...] = depth[last:]
    for copy in halos2:
        copy.start()

    surface = el + depth
    found = windows(surface)
    arrive_b()
    bed_s = recv_b[:, 0].reshape(slots, nodes)
    cpart_s = recv_b[:, 1].reshape(slots, nodes)
    width_s = recv_b[:, 2].reshape(slots, nodes)
    lateral2 = EXCHANGE_COEF * (bed_s + jnp.maximum(cpart_s - lateral * width_s, 0.0) - found)
    back_b[...] = lateral2.reshape(n, cpad, nodes)
    start_d()
    gained = gains(lateral2)

    fx = flood_x(fx, surface)
    fx_w[...] = fx
    for copy in halos2:
        copy.wait_recv()
    fy, top = flood_y(fy, top, surface, el_below + below2_r[...], el_above + above2_r[...])
    fy_w[...] = fy
    depth_w[...] = jnp.maximum(depth + inflow(fx, fy, top) + gained, 0.0)

    arrive_c()
    cdepth = jnp.maximum(
        cpart - per_width * pick(unpack, home_a[...].reshape(slots, nodes)), 0.0
    )
    cflow = channel_flow(cflow, bed + cdepth)
    cf_w[...] = cflow
    cpart = cdepth + channel_inflow(cflow)
    arrive_d()
    cd_w[...] = jnp.maximum(
        cpart - per_width * pick(unpack, home_b[...].reshape(slots, nodes)), 0.0
    )

    leave_a()
    leave_b()
    leave_c()
    leave_d()
    for copy in halos + halos2:
        copy.wait_send()


def write_out(*refs):
    copies = [pltpu.make_async_copy(refs[i], refs[5 + i], refs[10].at[i]) for i in range(5)]
    for copy in copies:
        copy.start()
    for copy in copies:
        copy.wait()


def per_device(
    depth, flux_x, flux_y, elevation, roughness, wet_tiles, chan_depth, chan_flow, chan_bed,
    chan_width, lateral_owner, lateral_row, reach_offset,
):
    n = lax.axis_size("rows")
    rows, columns = depth.shape
    reaches, nodes = chan_depth.shape
    cap = max(2, (3 * reaches + n - 1) // n)
    cpad = -(-(cap + 1) // 8) * 8
    operands = (
        depth, flux_x, flux_y, elevation, roughness, wet_tiles, chan_depth, chan_flow,
        chan_bed, chan_width, lateral_owner.reshape(1, reaches),
        lateral_row.reshape(1, reaches), reach_offset.reshape(1, reaches),
    )
    grid_like = jax.ShapeDtypeStruct((rows, columns), F32)
    chan_like = jax.ShapeDtypeStruct((reaches, nodes), F32)
    block = pltpu.VMEM((n, cpad, nodes), F32)
    triple = pltpu.VMEM((n, 3, cpad, nodes), F32)
    halo = pltpu.VMEM((5, columns), F32)
    line = pltpu.VMEM((1, columns), F32)
    dma = pltpu.SemaphoreType.DMA
    shapes = (grid_like, grid_like, grid_like, chan_like, chan_like)
    results = pl.pallas_call(
        functools.partial(kernel, n, cap, cpad),
        out_shape=shapes,
        in_specs=[pl.BlockSpec(memory_space=pltpu.HBM)] * len(operands),
        out_specs=[pl.BlockSpec(memory_space=pltpu.VMEM)] * 5,
        scratch_shapes=[pltpu.VMEM(x.shape, x.dtype) for x in operands]
        + [block, block, triple, triple, block, block, block, block]
        + [halo] * 4
        + [line] * 4
        + [dma((13,))]
        + [dma((n,))] * 8
        + [dma((4,)), dma((4,))],
        compiler_params=pltpu.CompilerParams(
            collective_id=0, has_side_effects=True, vmem_limit_bytes=24 * 1024 * 1024
        ),
    )(*[pltpu.with_memory_space_constraint(x, pltpu.HBM) for x in operands])
    return pl.pallas_call(
        write_out,
        out_shape=shapes,
        in_specs=[pl.BlockSpec(memory_space=pl.ANY)] * 5,
        out_specs=[pl.BlockSpec(memory_space=pltpu.HBM)] * 5,
        scratch_shapes=[dma((5,))],
        compiler_params=pltpu.CompilerParams(vmem_limit_bytes=4 * 1024 * 1024),
    )(*results)


def solution(mesh):
    spec2 = P(("groups", "rows"), None)
    spec1 = P(("groups", "rows"))
    return jax.shard_map(
        per_device,
        mesh=mesh,
        in_specs=(spec2,) * 11 + (spec1,) * 2,
        out_specs=(spec2,) * 5,
        check_vma=False,
    )
```

```python
import functools

import jax
import jax.numpy as jnp
from jax import lax
from jax.experimental import pallas as pl
from jax.experimental.pallas import tpu as pltpu
from jax.sharding import PartitionSpec as P

TILE = 8
LANES = 128

GRAVITY = 9.81
TIME_STEP = 5.0
CELL_SIZE = 90.0
DEPTH_FLOOR = 0.05
EXCHANGE_COEF = 40.0
CHANNEL_MANNING = 0.035

F32 = jnp.float32
BF16 = jnp.bfloat16
MESH = pl.DeviceIdType.MESH


def face_flux(flux, upper_a, upper_b, floor_a, floor_b, manning, active):
    flow_depth = jnp.maximum(jnp.maximum(upper_a, upper_b) - jnp.maximum(floor_a, floor_b), 0.0)
    slope = (upper_b - upper_a) * (GRAVITY * TIME_STEP / CELL_SIZE)
    inverse = jnp.exp((-7.0 / 3.0) * jnp.log(jnp.maximum(flow_depth, DEPTH_FLOOR)))
    return (
        active
        * (flux - flow_depth * slope)
        / (1.0 + (GRAVITY * TIME_STEP) * manning * manning * jnp.abs(flux) * inverse)
    )


def iota(shape, axis):
    return lax.broadcasted_iota(jnp.int32, shape, axis)


def split3(x):
    high = x.astype(BF16)
    rest = x - high.astype(F32)
    mid = rest.astype(BF16)
    low = (rest - mid.astype(F32)).astype(BF16)
    return jnp.concatenate([high, mid, low], axis=1)


def join3(x):
    width = x.shape[1] // 3
    return (x[:, 2 * width :] + x[:, width : 2 * width]) + x[:, :width]


def pick(onehot, x):
    return join3(jnp.dot(onehot, split3(x), preferred_element_type=F32))


def pick_t(onehot, x):
    return join3(
        lax.dot_general(
            onehot, split3(x), (((0,), (0,)), ((), ())), preferred_element_type=F32
        )
    )


def roll_rows(x, amount, to_right):
    source = iota(x.shape, 1) + (LANES - amount if to_right else amount)
    return jnp.take_along_axis(x, source & (LANES - 1), axis=1, mode="promise_in_bounds")


def kernel(n, cap, cpad, *refs):
    (
        depth_h, fx_h, fy_h, el_h, ro_h, wet_h, cd_h, cf_h, cb_h, cw_h, own_h, row_h, off_h,
        depth_w, fx_w, fy_w, cd_w, cf_w,
        depth_v, fx_v, fy_v, el_v, ro_v, wet_v, cd_v, cf_v, cb_v, cw_v, own_v, row_v, off_v,
        send_a, recv_a, send_b, recv_b, back_b, home_b,
        up_s, down_s, below_r, above_r, up2_s, down2_s, below2_r, above2_r,
        in_sem, sa, ra, sb, rb, sd, rd, hs, hr,
    ) = refs
    me = lax.axis_index("rows")
    rows, columns = depth_v.shape
    blocks = columns // LANES
    cells = rows * blocks
    reaches, nodes = cd_v.shape
    slots = n * cpad

    inputs = [
        pltpu.make_async_copy(h, v, in_sem.at[i])
        for i, (h, v) in enumerate(
            [
                (own_h, own_v), (row_h, row_v), (off_h, off_v), (cb_h, cb_v), (cd_h, cd_v),
                (depth_h, depth_v), (el_h, el_v), (ro_h, ro_v), (fy_h, fy_v), (wet_h, wet_v),
                (cf_h, cf_v), (cw_h, cw_v), (fx_h, fx_v),
            ]
        )
    ]
    for copy in inputs:
        copy.start()

    for ref in (recv_a, recv_b, home_b):
        ref[...] = jnp.zeros_like(ref)

    barrier = pltpu.get_barrier_semaphore()

    def greet(k, _):
        pl.semaphore_signal(
            barrier, inc=1, device_id={"rows": lax.rem(me + k, n)}, device_id_type=MESH
        )
        return _

    lax.fori_loop(1, n, greet, 0)

    for copy in inputs[:5]:
        copy.wait()
    owner_r = own_v[...]
    offset_r = off_v[...]
    key_r = (offset_r >> 7) * rows + row_v[...]
    turn_r = offset_r & (LANES - 1)
    ri, ci = iota((reaches, reaches), 0), iota((reaches, reaches), 1)

    def column(v):
        wide = jnp.broadcast_to(v.astype(F32), (reaches, reaches))
        return jnp.sum(jnp.where(ri == ci, wide, 0.0), axis=1, keepdims=True)

    owner_f = owner_r.astype(F32)
    owner_c, key_c, turn_c = column(owner_r), column(key_r), column(turn_r)
    same = jnp.where(owner_c == owner_f, 1.0, 0.0)
    rank_c = jnp.sum(jnp.where(ci < ri, same, 0.0), axis=1, keepdims=True)
    rank_r = jnp.sum(jnp.where(ri < ci, same, 0.0), axis=0, keepdims=True)
    slot_r = (owner_f * cpad + rank_r).astype(jnp.int32)
    slot_c = (owner_c * cpad + rank_c).astype(jnp.int32)
    pack = jnp.where(iota((slots, reaches), 0) == slot_r, 1.0, 0.0).astype(BF16)
    unpack = jnp.where(iota((reaches, slots), 1) == slot_c, 1.0, 0.0).astype(BF16)

    bed = cb_v[...]
    cdepth = cd_v[...]
    csurf = bed + cdepth
    send_a[...] = pick(pack, csurf).reshape(n, cpad, nodes)
    lane = iota((reaches, LANES), 1)
    rank_i = rank_c.astype(jnp.int32)
    ids = jnp.where(
        lane == rank_i, key_c + 1.0, jnp.where(lane == rank_i + 64, turn_c, 0.0)
    ).astype(BF16)
    to_owner = jnp.where(iota((n, reaches), 0) == owner_r, 1.0, 0.0).astype(BF16)
    id_rows = jnp.dot(to_owner, ids, preferred_element_type=F32)
    for d in range(n):
        send_a[d, cap : cap + 1, :] = id_rows[d : d + 1, :]

    for copy in inputs[5:10]:
        copy.wait()
    depth, el, ro = depth_v[...], el_v[...], ro_v[...]
    fy = fy_v[...]
    tiles = wet_v[...].astype(F32)
    last = rows - 1
    up_s[0:1, :] = depth[0:1]
    up_s[1:2, :] = el[0:1]
    up_s[2:3, :] = ro[0:1]
    up_s[3:4, :] = fy[0:1]
    up_s[4:5, :] = jnp.zeros((1, columns), F32)
    up_s[4:5, 0 : tiles.shape[1]] = tiles
    down_s[0:1, :] = depth[last:]
    down_s[1:2, :] = el[last:]
    down_s[2:3, :] = ro[last:]
    down_s[3:4, :] = fy[last:]
    down_s[4:5, :] = jnp.zeros((1, columns), F32)
    down_s[4:5, 0 : tiles.shape[1]] = tiles

    def exchange(source, target, span, send_sem, recv_sem):
        def make(k):
            peer = lax.rem(me + k, n)
            return pltpu.make_async_remote_copy(
                src_ref=source.at[(peer,) + span],
                dst_ref=target.at[(me,) + span],
                send_sem=send_sem.at[k],
                recv_sem=recv_sem.at[k],
                device_id={"rows": peer},
                device_id_type=MESH,
            )

        def start():
            def one(k, _):
                make(k).start()
                return _

            lax.fori_loop(1, n, one, 0)
            target[me] = source[me]

        def arrive():
            def one(k, _):
                make(k).wait_recv()
                return _

            lax.fori_loop(1, n, one, 0)

        def leave():
            def one(k, _):
                make(k).wait_send()
                return _

            lax.fori_loop(1, n, one, 0)

        return start, arrive, leave

    a_span = (pl.ds(0, cap + 1),)
    b_span = (slice(None), pl.ds(0, cap))
    start_a, arrive_a, leave_a = exchange(send_a, recv_a, a_span, sa, ra)
    start_b, arrive_b, leave_b = exchange(send_b, recv_b, b_span, sb, rb)
    start_d, arrive_d, leave_d = exchange(back_b, home_b, b_span, sd, rd)

    above, below = lax.rem(me + n - 1, n), lax.rem(me + 1, n)

    def halo(src, dst, i, peer):
        return pltpu.make_async_remote_copy(
            src_ref=src, dst_ref=dst, send_sem=hs.at[i], recv_sem=hr.at[i],
            device_id={"rows": peer}, device_id_type=MESH,
        )

    halos = [halo(up_s, below_r, 0, above), halo(down_s, above_r, 1, below)]
    halos2 = [halo(up2_s, below2_r, 2, above), halo(down2_s, above2_r, 3, below)]

    for copy in inputs[10:]:
        copy.wait()
    node = iota((reaches, nodes), 1)
    inner = jnp.where(node < nodes - 1, 1.0, 0.0)
    bed_next = pltpu.roll(bed, nodes - 1, 1)

    def channel_flow(flow, surface):
        return face_flux(
            flow, surface, pltpu.roll(surface, nodes - 1, 1), bed, bed_next,
            CHANNEL_MANNING, inner,
        )

    def channel_inflow(flow):
        return (TIME_STEP / CELL_SIZE) * (pltpu.roll(flow, 1, 1) - flow)

    cflow = channel_flow(cf_v[...], csurf)
    cpart = cdepth + channel_inflow(cflow)
    per_width = TIME_STEP / (cw_v[...] * CELL_SIZE)
    send_b[:, 0] = pick(pack, bed).reshape(n, cpad, nodes)
    send_b[:, 1] = pick(pack, cpart).reshape(n, cpad, nodes)
    send_b[:, 2] = pick(pack, per_width).reshape(n, cpad, nodes)
    pl.semaphore_wait(barrier, n - 1)
    start_a()
    for copy in halos:
        copy.start()
    start_b()

    col = iota((rows, columns), 1)
    row = iota((rows, columns), 0)
    spread = jnp.where(
        iota((tiles.shape[1], columns), 0) == iota((tiles.shape[1], columns), 1) // TILE, 1.0, 0.0
    ).astype(BF16)

    def expand(t):
        wide = jnp.broadcast_to(t, (rows, t.shape[1])).astype(BF16)
        return jnp.dot(wide, spread, preferred_element_type=F32)

    wet = expand(tiles)
    el_right = pltpu.roll(el, columns - 1, 1)
    man_x = 0.5 * (ro + pltpu.roll(ro, columns - 1, 1))
    act_x = jnp.where(
        col < columns - 1, jnp.maximum(wet, pltpu.roll(wet, columns - 1, 1)), 0.0
    )

    def flood_x(flux, surface):
        return face_flux(
            flux, surface, pltpu.roll(surface, columns - 1, 1), el, el_right, man_x, act_x
        )

    def to_cells(x):
        return jnp.concatenate([x[:, b * LANES : (b + 1) * LANES] for b in range(blocks)], axis=0)

    def to_grid(x):
        return jnp.concatenate([x[b * rows : (b + 1) * rows] for b in range(blocks)], axis=1)

    surface = el + depth
    fx = flood_x(fx_v[...], surface)

    for copy in halos:
        copy.wait_recv()

    def shift_up(x, edge):
        return jnp.where(row == last, edge, pltpu.roll(x, rows - 1, 0))

    def shift_down(x, edge):
        return jnp.where(row == 0, edge, pltpu.roll(x, 1, 0))

    edge_below = jnp.where(me == n - 1, 0.0, 1.0)
    edge_above = jnp.where(me == 0, 0.0, 1.0)
    wet_below = expand(below_r[4:5, 0 : tiles.shape[1]])
    wet_above = expand(above_r[4:5, 0 : tiles.shape[1]])[0:1]
    el_below = below_r[1:2, :]
    el_down = shift_up(el, el_below)
    man_y = 0.5 * (ro + shift_up(ro, below_r[2:3, :]))
    act_y = jnp.where(row == last, edge_below, 1.0) * jnp.maximum(wet, wet_below * 1.0)
    act_y = jnp.where(row == last, act_y, wet)
    el_above = above_r[1:2, :]
    man_top = 0.5 * (above_r[2:3, :] + ro[0:1])
    act_top = edge_above * jnp.maximum(wet_above, wet[0:1])

    def flood_y(flux, top, surface, below_row, above_row):
        new = face_flux(
            flux, surface, shift_up(surface, below_row), el, el_down, man_y, act_y
        )
        new_top = face_flux(top, above_row, surface[0:1], el_above, el[0:1], man_top, act_top)
        return new, new_top

    fy, top = flood_y(
        fy, above_r[3:4, :], surface, el_below + below_r[0:1, :], el_above + above_r[0:1, :]
    )

    def inflow(fx, fy, top):
        return (TIME_STEP / CELL_SIZE) * (
            pltpu.roll(fx, 1, 1) - fx + shift_down(fy, top) - fy
        )

    part = depth + inflow(fx, fy, top)

    arrive_a()
    packed = recv_a[...]
    wide_ids = jnp.broadcast_to(packed[:, cap : cap + 1, :], (n, cpad, LANES))
    mine = (iota((n, cpad, LANES), 2) & 63) == iota((n, cpad, LANES), 1)
    kept = jnp.where(mine, wide_ids, 0.0).reshape(slots, LANES).astype(BF16)
    halves = jnp.where(
        (iota((LANES, 2 * LANES), 0) < 64) == (iota((LANES, 2 * LANES), 1) < LANES), 1.0, 0.0
    ).astype(BF16)
    decoded = jnp.dot(kept, halves, preferred_element_type=F32).astype(jnp.int32)
    key = decoded[:, :LANES] - 1
    turn = decoded[:, LANES:]
    cell = iota((slots, cells), 1)
    key_cells = key[:, :cells]
    first = jnp.where(cell == key_cells, 1.0, 0.0).astype(BF16)
    second = jnp.where(
        (cell == key_cells + rows) & (key_cells >= 0), 1.0, 0.0
    ).astype(BF16)
    both = jnp.concatenate([first, second], axis=0)
    right = iota((slots, LANES), 1) >= turn

    def windows(surface):
        found = pick(both, to_cells(surface))
        return roll_rows(jnp.where(right, found[:slots], found[slots:]), turn, False)

    def gains(lateral):
        turned = roll_rows(lateral, turn, True)
        halves = jnp.concatenate(
            [jnp.where(right, turned, 0.0), jnp.where(right, 0.0, turned)], axis=0
        )
        return (TIME_STEP / (CELL_SIZE * CELL_SIZE)) * to_grid(pick_t(both, halves))

    csurf_s = packed.reshape(slots, nodes)
    lateral = EXCHANGE_COEF * (csurf_s - windows(surface))
    back_b[:, 0] = lateral.reshape(n, cpad, nodes)
    depth = jnp.maximum(part + gains(lateral), 0.0)
    up2_s[...] = depth[0:1]
    down2_s[...] = depth[last:]
    for copy in halos2:
        copy.start()

    surface = el + depth
    found = windows(surface)
    arrive_b()
    bed_s = recv_b[:, 0].reshape(slots, nodes)
    cpart_s = recv_b[:, 1].reshape(slots, nodes)
    width_s = recv_b[:, 2].reshape(slots, nodes)
    lateral2 = EXCHANGE_COEF * (bed_s + jnp.maximum(cpart_s - lateral * width_s, 0.0) - found)
    back_b[:, 1] = lateral2.reshape(n, cpad, nodes)
    start_d()
    gained = gains(lateral2)

    fx = flood_x(fx, surface)
    fx_w[...] = fx
    for copy in halos2:
        copy.wait_recv()
    fy, top = flood_y(fy, top, surface, el_below + below2_r[...], el_above + above2_r[...])
    fy_w[...] = fy
    depth_w[...] = jnp.maximum(depth + inflow(fx, fy, top) + gained, 0.0)

    arrive_d()
    cdepth = jnp.maximum(
        cpart - per_width * pick(unpack, home_b[:, 0].reshape(slots, nodes)), 0.0
    )
    cflow = channel_flow(cflow, bed + cdepth)
    cf_w[...] = cflow
    cpart = cdepth + channel_inflow(cflow)
    cd_w[...] = jnp.maximum(
        cpart - per_width * pick(unpack, home_b[:, 1].reshape(slots, nodes)), 0.0
    )

    leave_a()
    leave_b()
    leave_d()
    for copy in halos + halos2:
        copy.wait_send()


def write_out(*refs):
    copies = [pltpu.make_async_copy(refs[i], refs[5 + i], refs[10].at[i]) for i in range(5)]
    for copy in copies:
        copy.start()
    for copy in copies:
        copy.wait()


def per_device(
    depth, flux_x, flux_y, elevation, roughness, wet_tiles, chan_depth, chan_flow, chan_bed,
    chan_width, lateral_owner, lateral_row, reach_offset,
):
    n = lax.axis_size("rows")
    rows, columns = depth.shape
    reaches, nodes = chan_depth.shape
    cap = max(2, (3 * reaches + n - 1) // n)
    cpad = -(-(cap + 1) // 8) * 8
    operands = (
        depth, flux_x, flux_y, elevation, roughness, wet_tiles, chan_depth, chan_flow,
        chan_bed, chan_width, lateral_owner.reshape(1, reaches),
        lateral_row.reshape(1, reaches), reach_offset.reshape(1, reaches),
    )
    grid_like = jax.ShapeDtypeStruct((rows, columns), F32)
    chan_like = jax.ShapeDtypeStruct((reaches, nodes), F32)
    block = pltpu.VMEM((n, cpad, nodes), F32)
    double = pltpu.VMEM((n, 2, cpad, nodes), F32)
    triple = pltpu.VMEM((n, 3, cpad, nodes), F32)
    halo = pltpu.VMEM((5, columns), F32)
    line = pltpu.VMEM((1, columns), F32)
    dma = pltpu.SemaphoreType.DMA
    shapes = (grid_like, grid_like, grid_like, chan_like, chan_like)
    results = pl.pallas_call(
        functools.partial(kernel, n, cap, cpad),
        out_shape=shapes,
        in_specs=[pl.BlockSpec(memory_space=pltpu.HBM)] * len(operands),
        out_specs=[pl.BlockSpec(memory_space=pltpu.VMEM)] * 5,
        scratch_shapes=[pltpu.VMEM(x.shape, x.dtype) for x in operands]
        + [block, block, triple, triple, double, double]
        + [halo] * 4
        + [line] * 4
        + [dma((13,))]
        + [dma((n,))] * 6
        + [dma((4,)), dma((4,))],
        compiler_params=pltpu.CompilerParams(
            collective_id=0, has_side_effects=True, vmem_limit_bytes=24 * 1024 * 1024
        ),
    )(*[pltpu.with_memory_space_constraint(x, pltpu.HBM) for x in operands])
    return pl.pallas_call(
        write_out,
        out_shape=shapes,
        in_specs=[pl.BlockSpec(memory_space=pl.ANY)] * 5,
        out_specs=[pl.BlockSpec(memory_space=pltpu.HBM)] * 5,
        scratch_shapes=[dma((5,))],
        compiler_params=pltpu.CompilerParams(vmem_limit_bytes=4 * 1024 * 1024),
    )(*results)


def solution(mesh):
    spec2 = P(("groups", "rows"), None)
    spec1 = P(("groups", "rows"))
    return jax.shard_map(
        per_device,
        mesh=mesh,
        in_specs=(spec2,) * 11 + (spec1,) * 2,
        out_specs=(spec2,) * 5,
        check_vma=False,
    )
```

```python
import functools

import jax
import jax.numpy as jnp
from jax import lax
from jax.experimental import pallas as pl
from jax.experimental.pallas import tpu as pltpu
from jax.sharding import PartitionSpec as P

TILE = 8
LANES = 128

GRAVITY = 9.81
TIME_STEP = 5.0
CELL_SIZE = 90.0
DEPTH_FLOOR = 0.05
EXCHANGE_COEF = 40.0
CHANNEL_MANNING = 0.035

F32 = jnp.float32
BF16 = jnp.bfloat16
MESH = pl.DeviceIdType.MESH


def face_flux(flux, upper_a, upper_b, floor_a, floor_b, manning, active):
    flow_depth = jnp.maximum(jnp.maximum(upper_a, upper_b) - jnp.maximum(floor_a, floor_b), 0.0)
    slope = (upper_b - upper_a) * (GRAVITY * TIME_STEP / CELL_SIZE)
    inverse = jnp.exp((-7.0 / 3.0) * jnp.log(jnp.maximum(flow_depth, DEPTH_FLOOR)))
    return (
        active
        * (flux - flow_depth * slope)
        / (1.0 + (GRAVITY * TIME_STEP) * manning * manning * jnp.abs(flux) * inverse)
    )


def iota(shape, axis):
    return lax.broadcasted_iota(jnp.int32, shape, axis)


def split3(x):
    high = x.astype(BF16)
    rest = x - high.astype(F32)
    mid = rest.astype(BF16)
    low = (rest - mid.astype(F32)).astype(BF16)
    return jnp.concatenate([high, mid, low], axis=1)


def join3(x):
    width = x.shape[1] // 3
    return (x[:, 2 * width :] + x[:, width : 2 * width]) + x[:, :width]


def pick(onehot, x):
    return join3(jnp.dot(onehot, split3(x), preferred_element_type=F32))


def pick_t(onehot, x):
    return join3(
        lax.dot_general(
            onehot, split3(x), (((0,), (0,)), ((), ())), preferred_element_type=F32
        )
    )


def roll_rows(x, amount, to_right):
    source = iota(x.shape, 1) + (LANES - amount if to_right else amount)
    return jnp.take_along_axis(x, source & (LANES - 1), axis=1, mode="promise_in_bounds")


def kernel(n, cap, cpad, *refs):
    (
        depth_h, fx_h, fy_h, el_h, ro_h, wet_h, cd_h, cf_h, cb_h, cw_h, own_h, row_h, off_h,
        depth_w, fx_w, fy_w, cd_w, cf_w,
        depth_v, fx_v, fy_v, el_v, ro_v, wet_v, cd_v, cf_v, cb_v, cw_v, own_v, row_v, off_v,
        send_a, recv_a, send_b, recv_b, back_b, home_b,
        up_s, down_s, below_r, above_r, up2_s, down2_s, below2_r, above2_r,
        in_sem, sa, ra, sb, rb, sd, rd, hs, hr,
    ) = refs
    me = lax.axis_index("rows")
    rows, columns = depth_v.shape
    blocks = columns // LANES
    cells = rows * blocks
    reaches, nodes = cd_v.shape
    slots = n * cpad

    inputs = [
        pltpu.make_async_copy(h, v, in_sem.at[i])
        for i, (h, v) in enumerate(
            [
                (own_h, own_v), (row_h, row_v), (off_h, off_v), (cb_h, cb_v), (cd_h, cd_v),
                (depth_h, depth_v), (el_h, el_v), (ro_h, ro_v), (fy_h, fy_v), (wet_h, wet_v),
                (cf_h, cf_v), (cw_h, cw_v), (fx_h, fx_v),
            ]
        )
    ]
    for copy in inputs:
        copy.start()

    for ref in (recv_a, recv_b, home_b):
        ref[...] = jnp.zeros_like(ref)

    barrier = pltpu.get_barrier_semaphore()

    def greet(k, _):
        pl.semaphore_signal(
            barrier, inc=1, device_id={"rows": lax.rem(me + k, n)}, device_id_type=MESH
        )
        return _

    lax.fori_loop(1, n, greet, 0)

    for copy in inputs[:5]:
        copy.wait()
    owner_r = own_v[...]
    offset_r = off_v[...]
    key_r = (offset_r >> 7) * rows + row_v[...]
    turn_r = offset_r & (LANES - 1)
    ri, ci = iota((reaches, reaches), 0), iota((reaches, reaches), 1)

    def column(v):
        wide = jnp.broadcast_to(v.astype(F32), (reaches, reaches))
        return jnp.sum(jnp.where(ri == ci, wide, 0.0), axis=1, keepdims=True)

    owner_f = owner_r.astype(F32)
    owner_c, key_c, turn_c = column(owner_r), column(key_r), column(turn_r)
    same = jnp.where(owner_c == owner_f, 1.0, 0.0)
    rank_c = jnp.sum(jnp.where(ci < ri, same, 0.0), axis=1, keepdims=True)
    rank_r = jnp.sum(jnp.where(ri < ci, same, 0.0), axis=0, keepdims=True)
    slot_r = (owner_f * cpad + rank_r).astype(jnp.int32)
    slot_c = (owner_c * cpad + rank_c).astype(jnp.int32)
    pack = jnp.where(iota((slots, reaches), 0) == slot_r, 1.0, 0.0).astype(BF16)
    unpack = jnp.where(iota((reaches, slots), 1) == slot_c, 1.0, 0.0).astype(BF16)

    bed = cb_v[...]
    cdepth = cd_v[...]
    csurf = bed + cdepth
    send_a[...] = pick(pack, csurf).reshape(n, cpad, nodes)
    lane = iota((reaches, LANES), 1)
    rank_i = rank_c.astype(jnp.int32)
    ids = jnp.where(
        lane == rank_i, key_c + 1.0, jnp.where(lane == rank_i + 64, turn_c, 0.0)
    ).astype(BF16)
    to_owner = jnp.where(iota((n, reaches), 0) == owner_r, 1.0, 0.0).astype(BF16)
    id_rows = jnp.dot(to_owner, ids, preferred_element_type=F32)
    for d in range(n):
        send_a[d, cap : cap + 1, :] = id_rows[d : d + 1, :]

    for copy in inputs[5:10]:
        copy.wait()
    depth, el, ro = depth_v[...], el_v[...], ro_v[...]
    fy = fy_v[...]
    tiles = wet_v[...].astype(F32)
    last = rows - 1
    up_s[0:1, :] = depth[0:1]
    up_s[1:2, :] = el[0:1]
    up_s[2:3, :] = ro[0:1]
    up_s[3:4, :] = fy[0:1]
    up_s[4:5, :] = jnp.zeros((1, columns), F32)
    up_s[4:5, 0 : tiles.shape[1]] = tiles
    down_s[0:1, :] = depth[last:]
    down_s[1:2, :] = el[last:]
    down_s[2:3, :] = ro[last:]
    down_s[3:4, :] = fy[last:]
    down_s[4:5, :] = jnp.zeros((1, columns), F32)
    down_s[4:5, 0 : tiles.shape[1]] = tiles

    def exchange(source, target, span, send_sem, recv_sem):
        def make(k):
            peer = lax.rem(me + k, n)
            return pltpu.make_async_remote_copy(
                src_ref=source.at[(peer,) + span],
                dst_ref=target.at[(me,) + span],
                send_sem=send_sem.at[k],
                recv_sem=recv_sem.at[k],
                device_id={"rows": peer},
                device_id_type=MESH,
            )

        def start():
            def one(k, _):
                make(k).start()
                return _

            lax.fori_loop(1, n, one, 0, unroll=3)
            target[me] = source[me]

        def arrive():
            def one(k, _):
                make(k).wait_recv()
                return _

            lax.fori_loop(1, n, one, 0, unroll=3)

        def leave():
            def one(k, _):
                make(k).wait_send()
                return _

            lax.fori_loop(1, n, one, 0, unroll=3)

        return start, arrive, leave

    a_span = (pl.ds(0, cap + 1),)
    b_span = (slice(None), pl.ds(0, cap))
    start_a, arrive_a, leave_a = exchange(send_a, recv_a, a_span, sa, ra)
    start_b, arrive_b, leave_b = exchange(send_b, recv_b, b_span, sb, rb)
    start_d, arrive_d, leave_d = exchange(back_b, home_b, b_span, sd, rd)

    above, below = lax.rem(me + n - 1, n), lax.rem(me + 1, n)

    def halo(src, dst, i, peer):
        return pltpu.make_async_remote_copy(
            src_ref=src, dst_ref=dst, send_sem=hs.at[i], recv_sem=hr.at[i],
            device_id={"rows": peer}, device_id_type=MESH,
        )

    halos = [halo(up_s, below_r, 0, above), halo(down_s, above_r, 1, below)]
    halos2 = [halo(up2_s, below2_r, 2, above), halo(down2_s, above2_r, 3, below)]

    for copy in inputs[10:]:
        copy.wait()
    node = iota((reaches, nodes), 1)
    inner = jnp.where(node < nodes - 1, 1.0, 0.0)
    bed_next = pltpu.roll(bed, nodes - 1, 1)

    def channel_flow(flow, surface):
        return face_flux(
            flow, surface, pltpu.roll(surface, nodes - 1, 1), bed, bed_next,
            CHANNEL_MANNING, inner,
        )

    def channel_inflow(flow):
        return (TIME_STEP / CELL_SIZE) * (pltpu.roll(flow, 1, 1) - flow)

    cflow = channel_flow(cf_v[...], csurf)
    cpart = cdepth + channel_inflow(cflow)
    per_width = TIME_STEP / (cw_v[...] * CELL_SIZE)
    send_b[:, 0] = pick(pack, bed).reshape(n, cpad, nodes)
    send_b[:, 1] = pick(pack, cpart).reshape(n, cpad, nodes)
    send_b[:, 2] = pick(pack, per_width).reshape(n, cpad, nodes)
    pl.semaphore_wait(barrier, n - 1)
    start_a()
    for copy in halos:
        copy.start()
    start_b()

    col = iota((rows, columns), 1)
    row = iota((rows, columns), 0)
    spread = jnp.where(
        iota((tiles.shape[1], columns), 0) == iota((tiles.shape[1], columns), 1) // TILE, 1.0, 0.0
    ).astype(BF16)

    def expand(t):
        wide = jnp.broadcast_to(t, (rows, t.shape[1])).astype(BF16)
        return jnp.dot(wide, spread, preferred_element_type=F32)

    wet = expand(tiles)
    el_right = pltpu.roll(el, columns - 1, 1)
    man_x = 0.5 * (ro + pltpu.roll(ro, columns - 1, 1))
    act_x = jnp.where(
        col < columns - 1, jnp.maximum(wet, pltpu.roll(wet, columns - 1, 1)), 0.0
    )

    def flood_x(flux, surface):
        return face_flux(
            flux, surface, pltpu.roll(surface, columns - 1, 1), el, el_right, man_x, act_x
        )

    def to_cells(x):
        return jnp.concatenate([x[:, b * LANES : (b + 1) * LANES] for b in range(blocks)], axis=0)

    def to_grid(x):
        return jnp.concatenate([x[b * rows : (b + 1) * rows] for b in range(blocks)], axis=1)

    surface = el + depth
    fx = flood_x(fx_v[...], surface)

    for copy in halos:
        copy.wait_recv()

    def shift_up(x, edge):
        return jnp.where(row == last, edge, pltpu.roll(x, rows - 1, 0))

    def shift_down(x, edge):
        return jnp.where(row == 0, edge, pltpu.roll(x, 1, 0))

    edge_below = jnp.where(me == n - 1, 0.0, 1.0)
    edge_above = jnp.where(me == 0, 0.0, 1.0)
    wet_below = expand(below_r[4:5, 0 : tiles.shape[1]])
    wet_above = expand(above_r[4:5, 0 : tiles.shape[1]])[0:1]
    el_below = below_r[1:2, :]
    el_down = shift_up(el, el_below)
    man_y = 0.5 * (ro + shift_up(ro, below_r[2:3, :]))
    act_y = jnp.where(row == last, edge_below, 1.0) * jnp.maximum(wet, wet_below * 1.0)
    act_y = jnp.where(row == last, act_y, wet)
    el_above = above_r[1:2, :]
    man_top = 0.5 * (above_r[2:3, :] + ro[0:1])
    act_top = edge_above * jnp.maximum(wet_above, wet[0:1])

    def flood_y(flux, top, surface, below_row, above_row):
        new = face_flux(
            flux, surface, shift_up(surface, below_row), el, el_down, man_y, act_y
        )
        new_top = face_flux(top, above_row, surface[0:1], el_above, el[0:1], man_top, act_top)
        return new, new_top

    fy, top = flood_y(
        fy, above_r[3:4, :], surface, el_below + below_r[0:1, :], el_above + above_r[0:1, :]
    )

    def inflow(fx, fy, top):
        return (TIME_STEP / CELL_SIZE) * (
            pltpu.roll(fx, 1, 1) - fx + shift_down(fy, top) - fy
        )

    part = depth + inflow(fx, fy, top)

    arrive_a()
    packed = recv_a[...]
    wide_ids = jnp.broadcast_to(packed[:, cap : cap + 1, :], (n, cpad, LANES))
    mine = (iota((n, cpad, LANES), 2) & 63) == iota((n, cpad, LANES), 1)
    kept = jnp.where(mine, wide_ids, 0.0).reshape(slots, LANES).astype(BF16)
    halves = jnp.where(
        (iota((LANES, 2 * LANES), 0) < 64) == (iota((LANES, 2 * LANES), 1) < LANES), 1.0, 0.0
    ).astype(BF16)
    decoded = jnp.dot(kept, halves, preferred_element_type=F32).astype(jnp.int32)
    key = decoded[:, :LANES] - 1
    turn = decoded[:, LANES:]
    cell = iota((slots, cells), 1)
    key_cells = key[:, :cells]
    first = jnp.where(cell == key_cells, 1.0, 0.0).astype(BF16)
    second = jnp.where(
        (cell == key_cells + rows) & (key_cells >= 0), 1.0, 0.0
    ).astype(BF16)
    both = jnp.concatenate([first, second], axis=0)
    right = iota((slots, LANES), 1) >= turn

    def windows(surface):
        found = pick(both, to_cells(surface))
        return roll_rows(jnp.where(right, found[:slots], found[slots:]), turn, False)

    def gains(lateral):
        turned = roll_rows(lateral, turn, True)
        halves = jnp.concatenate(
            [jnp.where(right, turned, 0.0), jnp.where(right, 0.0, turned)], axis=0
        )
        return (TIME_STEP / (CELL_SIZE * CELL_SIZE)) * to_grid(pick_t(both, halves))

    csurf_s = packed.reshape(slots, nodes)
    lateral = EXCHANGE_COEF * (csurf_s - windows(surface))
    back_b[:, 0] = lateral.reshape(n, cpad, nodes)
    depth = jnp.maximum(part + gains(lateral), 0.0)
    up2_s[...] = depth[0:1]
    down2_s[...] = depth[last:]
    for copy in halos2:
        copy.start()

    surface = el + depth
    found = windows(surface)
    arrive_b()
    bed_s = recv_b[:, 0].reshape(slots, nodes)
    cpart_s = recv_b[:, 1].reshape(slots, nodes)
    width_s = recv_b[:, 2].reshape(slots, nodes)
    lateral2 = EXCHANGE_COEF * (bed_s + jnp.maximum(cpart_s - lateral * width_s, 0.0) - found)
    back_b[:, 1] = lateral2.reshape(n, cpad, nodes)
    start_d()
    gained = gains(lateral2)

    fx = flood_x(fx, surface)
    fx_w[...] = fx
    for copy in halos2:
        copy.wait_recv()
    fy, top = flood_y(fy, top, surface, el_below + below2_r[...], el_above + above2_r[...])
    fy_w[...] = fy
    depth_w[...] = jnp.maximum(depth + inflow(fx, fy, top) + gained, 0.0)

    arrive_d()
    cdepth = jnp.maximum(
        cpart - per_width * pick(unpack, home_b[:, 0].reshape(slots, nodes)), 0.0
    )
    cflow = channel_flow(cflow, bed + cdepth)
    cf_w[...] = cflow
    cpart = cdepth + channel_inflow(cflow)
    cd_w[...] = jnp.maximum(
        cpart - per_width * pick(unpack, home_b[:, 1].reshape(slots, nodes)), 0.0
    )

    leave_a()
    leave_b()
    leave_d()
    for copy in halos + halos2:
        copy.wait_send()


def write_out(*refs):
    copies = [pltpu.make_async_copy(refs[i], refs[5 + i], refs[10].at[i]) for i in range(5)]
    for copy in copies:
        copy.start()
    for copy in copies:
        copy.wait()


def per_device(
    depth, flux_x, flux_y, elevation, roughness, wet_tiles, chan_depth, chan_flow, chan_bed,
    chan_width, lateral_owner, lateral_row, reach_offset,
):
    n = lax.axis_size("rows")
    rows, columns = depth.shape
    reaches, nodes = chan_depth.shape
    cap = max(2, (3 * reaches + n - 1) // n)
    cpad = -(-(cap + 1) // 8) * 8
    operands = (
        depth, flux_x, flux_y, elevation, roughness, wet_tiles, chan_depth, chan_flow,
        chan_bed, chan_width, lateral_owner.reshape(1, reaches),
        lateral_row.reshape(1, reaches), reach_offset.reshape(1, reaches),
    )
    grid_like = jax.ShapeDtypeStruct((rows, columns), F32)
    chan_like = jax.ShapeDtypeStruct((reaches, nodes), F32)
    block = pltpu.VMEM((n, cpad, nodes), F32)
    double = pltpu.VMEM((n, 2, cpad, nodes), F32)
    triple = pltpu.VMEM((n, 3, cpad, nodes), F32)
    halo = pltpu.VMEM((5, columns), F32)
    line = pltpu.VMEM((1, columns), F32)
    dma = pltpu.SemaphoreType.DMA
    shapes = (grid_like, grid_like, grid_like, chan_like, chan_like)
    results = pl.pallas_call(
        functools.partial(kernel, n, cap, cpad),
        out_shape=shapes,
        in_specs=[pl.BlockSpec(memory_space=pltpu.HBM)] * len(operands),
        out_specs=[pl.BlockSpec(memory_space=pltpu.VMEM)] * 5,
        scratch_shapes=[pltpu.VMEM(x.shape, x.dtype) for x in operands]
        + [block, block, triple, triple, double, double]
        + [halo] * 4
        + [line] * 4
        + [dma((13,))]
        + [dma((n,))] * 6
        + [dma((4,)), dma((4,))],
        compiler_params=pltpu.CompilerParams(
            collective_id=0, has_side_effects=True, vmem_limit_bytes=24 * 1024 * 1024
        ),
    )(*[pltpu.with_memory_space_constraint(x, pltpu.HBM) for x in operands])
    return pl.pallas_call(
        write_out,
        out_shape=shapes,
        in_specs=[pl.BlockSpec(memory_space=pl.ANY)] * 5,
        out_specs=[pl.BlockSpec(memory_space=pltpu.HBM)] * 5,
        scratch_shapes=[dma((5,))],
        compiler_params=pltpu.CompilerParams(vmem_limit_bytes=4 * 1024 * 1024),
    )(*results)


def solution(mesh):
    spec2 = P(("groups", "rows"), None)
    spec1 = P(("groups", "rows"))
    return jax.shard_map(
        per_device,
        mesh=mesh,
        in_specs=(spec2,) * 11 + (spec1,) * 2,
        out_specs=(spec2,) * 5,
        check_vma=False,
    )
```
